512 devices in a mesh: seq: 64 (over y, x, core), tok: 8 (over z).
Axes of the slice: x: 4, y: 8, z: 8, core: 2. Of those that a mesh axis runs over, the one named last changes fastest.
Arguments:
- queries: bfloat16 [65536, 2048], P(('seq', 'tok')), may hold values from -6 to 6
- key_vectors: bfloat16 [65536, 2048], P(('seq', 'tok')), may hold values from -6 to 6
- value_vectors: bfloat16 [65536, 2048], P(('seq', 'tok')), may hold values from -6 to 6
- grad_output: bfloat16 [65536, 2048], P(('seq', 'tok')), may hold values from -8192 to 8192
- memory: float32 [64, 16, 128, 128], P('seq', 'tok'), may hold values from -7596.0074 to 7596.0074
- normalizer: float32 [64, 16, 128], P('seq', 'tok'), may hold values from 256 to 411648
- gate_logit: float32 [16], replicated, may hold values from 4 to 7
Outputs:
- grad_queries: bfloat16 [65536, 2048], P(('seq', 'tok'))
- grad_keys: bfloat16 [65536, 2048], P(('seq', 'tok'))
- grad_values: bfloat16 [65536, 2048], P(('seq', 'tok'))
The draws below stay inside these ranges and needn't reach their ends.
All inputs are finite; a program needn't handle non-finite values.
Results may differ from the reference program's by a relative error of at most 0.0022.
Values may be sent and summed in bfloat16 or wider, within the bound.
No kernel may reach another device: no remote copies, remote signals or barrier semaphores. Data moves between devices by JAX's collectives and lax.ppermute only.
A program may use at most 64 MiB of HBM per device.

```python
import jax
import jax.numpy as jnp
from jax import lax

HEADS = 16
HD = 128
SEG_LEN = 1024
TOKENS = 65536
N_SEQ = 64


def drawn_pair(key):
    row_count = TOKENS
    column_count = HEADS * HD
    first_key = jax.random.fold_in(key, 101)
    second_key = jax.random.fold_in(key, 202)
    query_out = jax.random.truncated_normal(first_key, -6.0, 6.0, (row_count, column_count))
    key_out = jax.random.truncated_normal(second_key, -6.0, 6.0, (row_count, column_count))
    return (query_out.astype(jnp.float32), key_out.astype(jnp.float32))


def draw_queries(key, part):
    return drawn_pair(key)[0].astype(jnp.bfloat16)


def draw_key_vectors(key, part):
    return drawn_pair(key)[1].astype(jnp.bfloat16)


def memory_state(key):
    offset = jax.random.uniform(jax.random.fold_in(key, 11), (), minval=1.0, maxval=4.0)
    log_coefficient = jax.random.uniform(jax.random.fold_in(key, 12), (HEADS, HD), minval=-0.693, maxval=1.386)
    column_scale = jnp.ones((HEADS, HD), jnp.float32)
    entries = jax.random.truncated_normal(jax.random.fold_in(key, 15), -6.0, 6.0, (N_SEQ, HEADS, HD, HD))
    coefficient = jnp.exp(log_coefficient)
    tokens_before = SEG_LEN * (jnp.arange(N_SEQ).astype(jnp.float32) + offset)
    jitter = 1.0 + 0.1 * jax.random.uniform(jax.random.fold_in(key, 13), (N_SEQ, HEADS, HD), minval=-1.0, maxval=1.0)
    normal_out = tokens_before[:, None, None] * coefficient[None] * jitter
    memory_out = jnp.sqrt(tokens_before)[:, None, None, None] * 1.2 * coefficient[None, :, :, None] * column_scale[None, :, None, :] * entries
    return (memory_out.astype(jnp.float32), normal_out.astype(jnp.float32))


def draw_memory(key, part):
    return memory_state(key)[0]


def draw_normalizer(key, part):
    return memory_state(key)[1]


def shard_levels(rng, extent, shards, least, top_value):
    factor_of, own = 1.0, jax.random.fold_in(rng, 6)
    for axis_at, blocks in shards:
        steps = jnp.exp(jax.random.uniform(jax.random.fold_in(own, axis_at), (blocks,), jnp.float32, least / len(shards), top_value / len(shards)))
        factor_of = factor_of * jnp.repeat(steps, extent[axis_at] // blocks).reshape([-1 if axis == axis_at else 1 for axis in range(len(extent))])
    return factor_of


def centred(rng, extent, deviation, most, pieces=(), held_as=jnp.bfloat16):
    values = deviation * jax.random.normal(rng, extent, jnp.float32)
    if pieces:
        values = values * shard_levels(rng, extent, pieces, -0.22, 0.18)
    return jnp.clip(values, -most, most).astype(held_as)


def setup_inputs(seed: int = 0) -> dict:
    seeds = jax.random.split(jax.random.key(seed), 8)
    return {
        "queries": draw_queries(jax.random.fold_in(seeds[7], 71), 0),
        "key_vectors": draw_key_vectors(jax.random.fold_in(seeds[7], 71), 0),
        "value_vectors": centred(seeds[2], (TOKENS, HEADS * HD), 1.0, 6.0, ((0, 512),)),
        "grad_output": centred(seeds[3], (TOKENS, HEADS * HD), 1024.0, 8192.0, ((0, 512),)),
        "memory": draw_memory(jax.random.fold_in(seeds[7], 71), 0),
        "normalizer": draw_normalizer(jax.random.fold_in(seeds[7], 71), 0),
        "gate_logit": jnp.clip(jax.random.uniform(seeds[6], (HEADS,), jnp.float32, 4.0, 7.0), 4.0, 7.0),
    }


HIGHEST = lax.Precision.HIGHEST
NEG_LARGE = -1e30


def feature_map(inputs):
    lower = jnp.exp(jnp.minimum(inputs, 0.0))
    positive = inputs > 0
    return jnp.where(positive, inputs + 1.0, lower), jnp.where(positive, 1.0, lower)


def memory_read(query_rows, grad_rows, memory_slab, normal_vector, gate_value):
    features, slopes = feature_map(query_rows.astype(jnp.float32))
    numerator = jnp.dot(features, memory_slab, precision=HIGHEST)
    denominator = jnp.dot(features, normal_vector, precision=HIGHEST)
    scaled_grad = gate_value * grad_rows.astype(jnp.float32)
    grad_numerator = scaled_grad / denominator[:, None]
    grad_denominator = -jnp.sum(scaled_grad * numerator, axis=1) / (denominator * denominator)
    memory_grad = jnp.dot(features.T, grad_numerator, precision=HIGHEST)
    normal_grad = jnp.dot(grad_denominator, features, precision=HIGHEST)
    grad_features = jnp.dot(grad_numerator, memory_slab.T, precision=HIGHEST) + grad_denominator[:, None] * normal_vector[None, :]
    return memory_grad, normal_grad, grad_features * slopes


def memory_write(key_rows, value_rows, later_memory, later_normal):
    features, slopes = feature_map(key_rows.astype(jnp.float32))
    value_grad = jnp.dot(features, later_memory, precision=HIGHEST)
    feature_grad = jnp.dot(value_rows.astype(jnp.float32), later_memory.T, precision=HIGHEST) + later_normal[None, :]
    return feature_grad * slopes, value_grad


def attend_rows(query_rows, row_start, key_rows, value_rows, grad_rows, local_share, score_scale):
    scores = jnp.einsum('qd,kd->qk', query_rows, key_rows, preferred_element_type=jnp.float32) * score_scale
    positions = row_start + lax.broadcasted_iota(jnp.int32, scores.shape, 0)
    columns = lax.broadcasted_iota(jnp.int32, scores.shape, 1)
    scores = jnp.where(columns <= positions, scores, NEG_LARGE)
    highest = jnp.max(scores, axis=1, keepdims=True)
    exponent = jnp.exp(scores - highest)
    attention = exponent / jnp.sum(exponent, axis=1, keepdims=True)
    grad_attention = local_share * jnp.einsum('qd,kd->qk', grad_rows, value_rows, preferred_element_type=jnp.float32)
    centre = jnp.sum(attention * grad_attention, axis=1, keepdims=True)
    grad_scores = (attention * (grad_attention - centre)).astype(jnp.bfloat16)
    grad_query = score_scale * jnp.dot(grad_scores, key_rows, preferred_element_type=jnp.float32)
    grad_key = score_scale * jnp.einsum('qk,qd->kd', grad_scores, query_rows, preferred_element_type=jnp.float32)
    grad_value = local_share * jnp.einsum('qk,qd->kd', attention.astype(jnp.bfloat16), grad_rows, preferred_element_type=jnp.float32)
    return grad_query, grad_key, grad_value


def reference(queries, key_vectors, value_vectors, grad_output, memory, normalizer, gate_logit):
    def heads_first(array):
        return array.reshape(N_SEQ, SEG_LEN, HEADS, HD).transpose(0, 2, 1, 3).reshape(N_SEQ * HEADS, SEG_LEN, HD)

    query_all = heads_first(queries)
    key_all = heads_first(key_vectors)
    value_all = heads_first(value_vectors)
    grad_all = heads_first(grad_output)
    gate_all = jnp.tile(jax.nn.sigmoid(gate_logit), N_SEQ)
    memory_all = memory.reshape(N_SEQ * HEADS, HD, HD)
    normal_all = normalizer.reshape(N_SEQ * HEADS, HD)

    def first_pass(items):
        query_rows, grad_rows, memory_slab, normal_vector, gate_value = items
        memory_grad, normal_grad, unused = memory_read(query_rows, grad_rows, memory_slab, normal_vector, gate_value)
        return memory_grad, normal_grad

    memory_grads, normal_grads = lax.map(first_pass, (query_all, grad_all, memory_all, normal_all, gate_all))

    def suffix_sum(array):
        running = jnp.cumsum(array[::-1], axis=0)[::-1]
        return jnp.concatenate([running[1:], jnp.zeros_like(running[:1])], axis=0)

    later_memory = suffix_sum(memory_grads.reshape(N_SEQ, HEADS, HD, HD)).reshape(N_SEQ * HEADS, HD, HD)
    later_normal = suffix_sum(normal_grads.reshape(N_SEQ, HEADS, HD)).reshape(N_SEQ * HEADS, HD)
    score_scale = HD ** -0.5

    def second_pass(items):
        query_rows, key_rows, value_rows, grad_rows, memory_slab, normal_vector, gate_value, memory_later, normal_later = items
        unused_one, unused_two, query_memory = memory_read(query_rows, grad_rows, memory_slab, normal_vector, gate_value)
        grad_query, grad_key, grad_value = attend_rows(query_rows, 0, key_rows, value_rows, grad_rows, 1.0 - gate_value, score_scale)
        key_write, value_write = memory_write(key_rows, value_rows, memory_later, normal_later)
        return ((grad_query + query_memory).astype(jnp.bfloat16), (grad_key + key_write).astype(jnp.bfloat16), (grad_value + value_write).astype(jnp.bfloat16))

    grad_q, grad_k, grad_v = lax.map(second_pass, (query_all, key_all, value_all, grad_all, memory_all, normal_all, gate_all, later_memory, later_normal))

    def tokens_first(array):
        return array.reshape(N_SEQ, HEADS, SEG_LEN, HD).transpose(0, 2, 1, 3).reshape(TOKENS, HEADS * HD)

    return (tokens_first(grad_q), tokens_first(grad_k), tokens_first(grad_v))
```

```python
import functools

import jax
import jax.numpy as jnp
from jax import lax
from jax.experimental import pallas as pl
from jax.experimental.pallas import tpu as pltpu
from jax.sharding import PartitionSpec as P

SEQ_GRID = (8, 4)
LOG2E = 1.4426950408889634
VMEM_LIMIT = 48 * 1024 * 1024
F32 = jnp.float32
BF16 = jnp.bfloat16


def params():
    return pltpu.CompilerParams(vmem_limit_bytes=VMEM_LIMIT)


def cost(flops, moved):
    return pl.CostEstimate(flops=int(flops), bytes_accessed=int(moved), transcendentals=0)


def split(value):
    high = value.astype(BF16)
    return high, (value - high.astype(F32)).astype(BF16)


def dot(left, right, left_dim=1, right_dim=0):
    return lax.dot_general(
        left, right, (((left_dim,), (right_dim,)), ((), ())), preferred_element_type=F32
    )


def dot3(left, right, left_dim=1, right_dim=0):
    (lh, ll), (rh, rl) = left, right
    return (
        dot(lh, rh, left_dim, right_dim)
        + dot(lh, rl, left_dim, right_dim)
        + dot(ll, rh, left_dim, right_dim)
    )


def feature_map(inputs):
    lower = jnp.exp(jnp.minimum(inputs, 0.0))
    positive = inputs > 0
    return jnp.where(positive, inputs + 1.0, lower), jnp.where(positive, 1.0, lower)


def rows_of(block):
    return block.reshape(block.shape[0] * block.shape[1], block.shape[2])


def pack_kernel(count, *refs):
    sources, (target, sems) = refs[:count], refs[count:]
    groups, _, _, width = target.shape
    copies = []
    for group in range(groups):
        for which, source in enumerate(sources):
            copies.append(
                pltpu.make_async_copy(
                    source.at[:, pl.ds(group * width, width)],
                    target.at[group, which],
                    sems.at[group * count + which],
                )
            )
    for copy in copies:
        copy.start()
    for copy in copies:
        copy.wait()


def pack(arrays, groups):
    rows, columns = arrays[0].shape
    count = len(arrays)
    return pl.pallas_call(
        functools.partial(pack_kernel, count),
        out_shape=jax.ShapeDtypeStruct((groups, count, rows, columns // groups), arrays[0].dtype),
        in_specs=[pl.BlockSpec(memory_space=pl.ANY)] * count,
        out_specs=pl.BlockSpec(memory_space=pltpu.VMEM),
        scratch_shapes=[pltpu.SemaphoreType.DMA((groups * count,))],
        cost_estimate=cost(0, 4 * count * rows * columns),
        name="pack",
    )(*arrays)


def unpack_kernel(count, source, *refs):
    targets, sems = refs[:count], refs[count]
    groups, _, _, width = source.shape
    copies = []
    for group in range(groups):
        for which, target in enumerate(targets):
            copies.append(
                pltpu.make_async_copy(
                    source.at[group, which],
                    target.at[:, pl.ds(group * width, width)],
                    sems.at[group * count + which],
                )
            )
    for copy in copies:
        copy.start()
    for copy in copies:
        copy.wait()


def unpack(array):
    groups, count, rows, width = array.shape
    return pl.pallas_call(
        functools.partial(unpack_kernel, count),
        out_shape=[jax.ShapeDtypeStruct((rows, groups * width), array.dtype)] * count,
        in_specs=[pl.BlockSpec(array.shape, lambda: (0, 0, 0, 0))],
        out_specs=[pl.BlockSpec(memory_space=pl.ANY)] * count,
        scratch_shapes=[pltpu.SemaphoreType.DMA((groups * count,))],
        cost_estimate=cost(0, 4 * array.size),
        name="unpack",
    )(array)


def read_kernel(gate_ref, both_ref, memory_ref, normal_ref, sums_ref, part_ref):
    gate = gate_ref[pl.program_id(0)]
    query = rows_of(both_ref[:, 0]).astype(F32)
    grad = rows_of(both_ref[:, 1]).astype(F32)
    memory = memory_ref[0]
    normal = normal_ref[0]
    size = memory.shape[0]
    features, slopes = feature_map(query)
    features2 = split(features)
    memory2 = split(memory)
    numerator = dot3(features2, memory2)
    inverse = 1.0 / jnp.sum(features * normal, axis=1, keepdims=True)
    scaled = gate * grad
    grad_numerator = scaled * inverse
    grad_denominator = -jnp.sum(scaled * numerator, axis=1, keepdims=True) * inverse * inverse
    numerator2 = split(grad_numerator)
    sums_ref[0, :size, :] = dot3(features2, numerator2, 0, 0)
    normal_grad = jnp.sum(features * grad_denominator, axis=0, keepdims=True)
    sums_ref[0, size:, :] = jnp.broadcast_to(normal_grad, (8, size))
    part_ref[...] = (dot3(numerator2, memory2, 1, 1) + grad_denominator * normal) * slopes


def memory_read(gates, both, memory, normalizer):
    groups, _, rows, width = both.shape
    heads, size, _ = memory.shape
    return pl.pallas_call(
        read_kernel,
        grid=(heads,),
        out_shape=[
            jax.ShapeDtypeStruct((heads, size + 8, size), F32),
            jax.ShapeDtypeStruct((groups * rows, width), F32),
        ],
        in_specs=[
            pl.BlockSpec(memory_space=pltpu.SMEM),
            pl.BlockSpec((groups, 2, rows, size), lambda h: (0, 0, 0, h)),
            pl.BlockSpec((1, size, size), lambda h: (h, 0, 0)),
            pl.BlockSpec((1, 1, size), lambda h: (h, 0, 0)),
        ],
        out_specs=[
            pl.BlockSpec((1, size + 8, size), lambda h: (h, 0, 0)),
            pl.BlockSpec((groups * rows, size), lambda h: (0, h)),
        ],
        compiler_params=params(),
        cost_estimate=cost(heads * 9 * 2 * groups * rows * size * size * 2, 4e6),
        name="memory_read",
    )(gates, both, memory, normalizer)


def attend_kernel(block, head, gate_ref, qo_ref, kv_ref, part_ref, dq_ref, dk_ref, dv_ref):
    local_share = 1.0 - gate_ref[head]
    query = rows_of(qo_ref[:, 0])
    grad = rows_of(qo_ref[:, 1])
    key = rows_of(kv_ref[:, 0])
    value = rows_of(kv_ref[:, 1])
    total, size = query.shape
    scale = size**-0.5
    for start in range(0, total, block):
        count = start + block
        q = query[start:count]
        o = grad[start:count]
        k = key[:count]
        scores = dot(k, q, 1, 1)
        diagonal = scores[start:]
        keep = lax.broadcasted_iota(jnp.int32, diagonal.shape, 0) <= lax.broadcasted_iota(
            jnp.int32, diagonal.shape, 1
        )
        diagonal = jnp.where(keep, diagonal, -1e30)
        scores = jnp.concatenate([scores[:start], diagonal], axis=0) if start else diagonal
        highest = jnp.max(scores, axis=0, keepdims=True)
        factor = scale * LOG2E
        weights = jnp.exp2(scores * factor - highest * factor)
        inverse = 1.0 / jnp.sum(weights, axis=0, keepdims=True)
        moved = dot(value[:count], o, 1, 1)
        centre = jnp.sum(weights * moved, axis=0, keepdims=True) * inverse
        attention = (weights * inverse).astype(BF16)
        grad_scores = (weights * (inverse * local_share) * (moved - centre)).astype(BF16)
        grad_query = dot(grad_scores, k, 0, 0)
        dq_ref[start:count, :] = (scale * grad_query + part_ref[start:count, :]).astype(BF16)
        grad_key = scale * dot(grad_scores, q)
        grad_value = local_share * dot(attention, o)
        if start:
            dk_ref[:start, :] += grad_key[:start]
            dv_ref[:start, :] += grad_value[:start]
        dk_ref[start:count, :] = grad_key[start:]
        dv_ref[start:count, :] = grad_value[start:]


def attend(head, gates, qo, kv, part):
    groups, _, rows, width = qo.shape
    total = groups * rows
    size = width // gates.shape[0]
    four = pl.BlockSpec((groups, 2, rows, size), lambda i: (0, 0, 0, head))
    flat = pl.BlockSpec((total, size), lambda i: (0, 0))
    return pl.pallas_call(
        functools.partial(attend_kernel, min(256, total), head),
        grid=(1,),
        out_shape=[
            jax.ShapeDtypeStruct((total, size), BF16),
            jax.ShapeDtypeStruct((total, size), F32),
            jax.ShapeDtypeStruct((total, size), F32),
        ],
        in_specs=[
            pl.BlockSpec(memory_space=pltpu.SMEM),
            four,
            four,
            pl.BlockSpec((total, size), lambda i: (0, head)),
        ],
        out_specs=[flat, flat, flat],
        compiler_params=params(),
        cost_estimate=cost(16 * total * total * size, 4e6),
        name="attend",
    )(gates, qo, kv, part)


def write_kernel(kv_ref, later_ref, *refs):
    heads, padded, size = later_ref.shape
    parts, out_ref = refs[:-1], refs[-1]
    groups, _, rows, _ = out_ref.shape
    for head in range(heads):
        columns = pl.ds(head * size, size)
        dq_ref, dk_ref, dv_ref = parts[3 * head : 3 * head + 3]
        key = rows_of(kv_ref[:, 0, :, columns]).astype(F32)
        value = rows_of(kv_ref[:, 1, :, columns])
        later = split(later_ref[head, :size, :])
        later_normal = later_ref[head, size : size + 1, :]
        features, slopes = feature_map(key)
        high, low = later
        grad_features = dot(value, high, 1, 1) + dot(value, low, 1, 1) + later_normal
        grad_key = dk_ref[...] + grad_features * slopes
        grad_value = dv_ref[...] + dot3(split(features), later)
        out_ref[:, 0, :, columns] = dq_ref[...].reshape(groups, rows, size)
        out_ref[:, 1, :, columns] = grad_key.astype(BF16).reshape(groups, rows, size)
        out_ref[:, 2, :, columns] = grad_value.astype(BF16).reshape(groups, rows, size)


def memory_write(kv, later, parts):
    groups, _, rows, width = kv.shape
    heads, padded, size = later.shape
    return pl.pallas_call(
        write_kernel,
        out_shape=jax.ShapeDtypeStruct((groups, 3, rows, width), BF16),
        compiler_params=params(),
        cost_estimate=cost(heads * 5 * 2 * groups * rows * size * size * 2, 4e6),
        name="memory_write",
    )(kv, later, *parts)


def later_sums(sums, rows, columns):
    me = lax.axis_index("seq")
    second = me % 2 == 1
    line = 2 * columns

    def send(value, pairs):
        return lax.ppermute(value, "seq", pairs)

    def swap(value):
        return send(value, [(i, i ^ 1) for i in range(rows * line)])

    mine = jnp.where(second, sums[1], sums[0])
    other = jnp.where(second, sums[0], sums[1])
    received = swap(other)
    chip = mine + received
    below = None
    step = 1
    while step < rows:
        sent = chip if below is None else chip + below
        got = send(sent, [(i, i - step * line) for i in range(step * line, rows * line)])
        below = got if below is None else below + got
        step *= 2
    column = (me // 2) % columns
    whole = chip + below
    later = below
    for shift in range(1, columns):
        value = jnp.where(column >= shift, whole, below)
        pairs = [
            ((r * columns + c) * 2 + k, (r * columns + (c - shift) % columns) * 2 + k)
            for r in range(rows)
            for c in range(columns)
            for k in range(2)
        ]
        later = later + send(value, pairs)
    returned = swap(jnp.where(second, later + mine, later))
    kept = jnp.where(second, later, later + received)
    return jnp.where(second, jnp.stack([returned, kept]), jnp.stack([kept, returned]))


def exchange(array):
    return lax.all_to_all(array, "tok", split_axis=0, concat_axis=0, tiled=True)


def body(queries, key_vectors, value_vectors, grad_output, memory, normalizer, gate_logit):
    groups = lax.axis_size("tok")
    heads = gate_logit.shape[0] // groups
    gates = jax.nn.sigmoid(
        lax.dynamic_slice_in_dim(gate_logit, lax.axis_index("tok") * heads, heads)
    )
    qo = exchange(pack([queries, grad_output], groups))
    kv = exchange(pack([key_vectors, value_vectors], groups))
    sums, part = memory_read(gates, qo, memory[0], normalizer[0][:, None, :])
    later = later_sums(sums, *SEQ_GRID)
    parts = [value for head in range(heads) for value in attend(head, gates, qo, kv, part)]
    return tuple(unpack(exchange(memory_write(kv, later, parts))))


def solution(mesh):
    in_specs = (
        P(("seq", "tok"), None),
        P(("seq", "tok"), None),
        P(("seq", "tok"), None),
        P(("seq", "tok"), None),
        P("seq", "tok", None, None),
        P("seq", "tok", None),
        P(),
    )
    out_specs = (P(("seq", "tok"), None), P(("seq", "tok"), None), P(("seq", "tok"), None))
    return jax.shard_map(body, mesh=mesh, in_specs=in_specs, out_specs=out_specs, check_vma=False)
```

```python
import functools

import jax
import jax.numpy as jnp
from jax import lax
from jax.experimental import pallas as pl
from jax.experimental.pallas import tpu as pltpu
from jax.sharding import PartitionSpec as P

SEQ_GRID = (8, 4)
LOG2E = 1.4426950408889634
VMEM_LIMIT = 24 * 1024 * 1024
F32 = jnp.float32
BF16 = jnp.bfloat16


def params():
    return pltpu.CompilerParams(vmem_limit_bytes=VMEM_LIMIT)


def cost(flops, moved):
    return pl.CostEstimate(flops=int(flops), bytes_accessed=int(moved), transcendentals=0)


def split(value):
    high = value.astype(BF16)
    return high, (value - high.astype(F32)).astype(BF16)


def dot(left, right, left_dim=1, right_dim=0):
    return lax.dot_general(
        left, right, (((left_dim,), (right_dim,)), ((), ())), preferred_element_type=F32
    )


def dot3(left, right, left_dim=1, right_dim=0):
    (lh, ll), (rh, rl) = left, right
    return (
        dot(lh, rh, left_dim, right_dim)
        + dot(lh, rl, left_dim, right_dim)
        + dot(ll, rh, left_dim, right_dim)
    )


def feature_map(inputs):
    lower = jnp.exp(jnp.minimum(inputs, 0.0))
    positive = inputs > 0
    return jnp.where(positive, inputs + 1.0, lower), jnp.where(positive, 1.0, lower)


def gate_of(gates_ref, head):
    gates = gates_ref[...]
    at = lax.broadcasted_iota(jnp.int32, gates.shape, 1) == head
    return jnp.sum(jnp.where(at, gates, 0.0), axis=1, keepdims=True)


def rows_of(block):
    return block.reshape(block.shape[0] * block.shape[1], block.shape[2])


def pack_kernel(count, *refs):
    sources, (target, sems) = refs[:count], refs[count:]
    groups, _, _, width = target.shape
    copies = []
    for group in range(groups):
        for which, source in enumerate(sources):
            copies.append(
                pltpu.make_async_copy(
                    source.at[:, pl.ds(group * width, width)],
                    target.at[group, which],
                    sems.at[group * count + which],
                )
            )
    for copy in copies:
        copy.start()
    for copy in copies:
        copy.wait()


def pack(arrays, groups):
    rows, columns = arrays[0].shape
    count = len(arrays)
    return pl.pallas_call(
        functools.partial(pack_kernel, count),
        out_shape=jax.ShapeDtypeStruct((groups, count, rows, columns // groups), arrays[0].dtype),
        in_specs=[pl.BlockSpec(memory_space=pl.ANY)] * count,
        out_specs=pl.BlockSpec(memory_space=pltpu.VMEM),
        scratch_shapes=[pltpu.SemaphoreType.DMA((groups * count,))],
        cost_estimate=cost(0, 4 * count * rows * columns),
        name="pack",
    )(*arrays)


def unpack_kernel(count, source, *refs):
    targets, sems = refs[:count], refs[count]
    groups, _, _, width = source.shape
    copies = []
    for group in range(groups):
        for which, target in enumerate(targets):
            copies.append(
                pltpu.make_async_copy(
                    source.at[group, which],
                    target.at[:, pl.ds(group * width, width)],
                    sems.at[group * count + which],
                )
            )
    for copy in copies:
        copy.start()
    for copy in copies:
        copy.wait()


def unpack(array):
    groups, count, rows, width = array.shape
    return pl.pallas_call(
        functools.partial(unpack_kernel, count),
        out_shape=[jax.ShapeDtypeStruct((rows, groups * width), array.dtype)] * count,
        in_specs=[pl.BlockSpec(array.shape, lambda: (0, 0, 0, 0))],
        out_specs=[pl.BlockSpec(memory_space=pl.ANY)] * count,
        scratch_shapes=[pltpu.SemaphoreType.DMA((groups * count,))],
        cost_estimate=cost(0, 4 * array.size),
        name="unpack",
    )(array)


def read_kernel(gates_ref, both_ref, memory_ref, normal_ref, sums_ref, part_ref):
    gate = gate_of(gates_ref, pl.program_id(0))
    query = rows_of(both_ref[:, 0]).astype(F32)
    grad = rows_of(both_ref[:, 1]).astype(F32)
    memory = memory_ref[0]
    normal = normal_ref[0]
    size = memory.shape[0]
    features, slopes = feature_map(query)
    features2 = split(features)
    memory2 = split(memory)
    numerator = dot3(features2, memory2)
    inverse = 1.0 / jnp.sum(features * normal, axis=1, keepdims=True)
    scaled = gate * grad
    grad_numerator = scaled * inverse
    grad_denominator = -jnp.sum(scaled * numerator, axis=1, keepdims=True) * inverse * inverse
    numerator2 = split(grad_numerator)
    sums_ref[0, :size, :] = dot3(features2, numerator2, 0, 0)
    normal_grad = jnp.sum(features * grad_denominator, axis=0, keepdims=True)
    sums_ref[0, size:, :] = jnp.broadcast_to(normal_grad, (8, size))
    part_ref[...] = (dot3(numerator2, memory2, 1, 1) + grad_denominator * normal) * slopes


def memory_read(gates, both, memory, normalizer):
    groups, _, rows, width = both.shape
    heads, size, _ = memory.shape
    return pl.pallas_call(
        read_kernel,
        grid=(heads,),
        out_shape=[
            jax.ShapeDtypeStruct((heads, size + 8, size), F32),
            jax.ShapeDtypeStruct((groups * rows, width), F32),
        ],
        in_specs=[
            pl.BlockSpec(gates.shape, lambda i: (0, 0)),
            pl.BlockSpec((groups, 2, rows, size), lambda h: (0, 0, 0, h)),
            pl.BlockSpec((1, size, size), lambda h: (h, 0, 0)),
            pl.BlockSpec((1, 1, size), lambda h: (h, 0, 0)),
        ],
        out_specs=[
            pl.BlockSpec((1, size + 8, size), lambda h: (h, 0, 0)),
            pl.BlockSpec((groups * rows, size), lambda h: (0, h)),
        ],
        compiler_params=params(),
        cost_estimate=cost(heads * 9 * 2 * groups * rows * size * size * 2, 4e6),
        name="memory_read",
    )(gates, both, memory, normalizer)


def attend_kernel(block, head, gates_ref, qo_ref, kv_ref, part_ref, dq_ref, dk_ref, dv_ref):
    local_share = 1.0 - gate_of(gates_ref, head)
    query = rows_of(qo_ref[:, 0])
    grad = rows_of(qo_ref[:, 1])
    key = rows_of(kv_ref[:, 0])
    value = rows_of(kv_ref[:, 1])
    total, size = query.shape
    scale = size**-0.5
    for start in range(0, total, block):
        count = start + block
        q = query[start:count]
        o = grad[start:count]
        k = key[:count]
        scores = dot(k, q, 1, 1)
        diagonal = scores[start:]
        keep = lax.broadcasted_iota(jnp.int32, diagonal.shape, 0) <= lax.broadcasted_iota(
            jnp.int32, diagonal.shape, 1
        )
        diagonal = jnp.where(keep, diagonal, -1e30)
        scores = jnp.concatenate([scores[:start], diagonal], axis=0) if start else diagonal
        highest = jnp.max(scores, axis=0, keepdims=True)
        factor = scale * LOG2E
        weights = jnp.exp2(scores * factor - highest * factor)
        inverse = 1.0 / jnp.sum(weights, axis=0, keepdims=True)
        moved = dot(value[:count], o, 1, 1)
        centre = jnp.sum(weights * moved, axis=0, keepdims=True) * inverse
        attention = (weights * inverse).astype(BF16)
        grad_scores = (weights * (inverse * local_share) * (moved - centre)).astype(BF16)
        grad_query = dot(grad_scores, k, 0, 0)
        dq_ref[start:count, :] = (scale * grad_query + part_ref[start:count, :]).astype(BF16)
        grad_key = scale * dot(grad_scores, q)
        grad_value = local_share * dot(attention, o)
        if start:
            dk_ref[:start, :] += grad_key[:start]
            dv_ref[:start, :] += grad_value[:start]
        dk_ref[start:count, :] = grad_key[start:]
        dv_ref[start:count, :] = grad_value[start:]


def attend(head, gates, qo, kv, part):
    groups, _, rows, width = qo.shape
    total = groups * rows
    size = width // gates.shape[1]
    four = pl.BlockSpec((groups, 2, rows, size), lambda i: (0, 0, 0, head))
    flat = pl.BlockSpec((total, size), lambda i: (0, 0))
    return pl.pallas_call(
        functools.partial(attend_kernel, min(256, total), head),
        grid=(1,),
        out_shape=[
            jax.ShapeDtypeStruct((total, size), BF16),
            jax.ShapeDtypeStruct((total, size), F32),
            jax.ShapeDtypeStruct((total, size), F32),
        ],
        in_specs=[
            pl.BlockSpec(gates.shape, lambda i: (0, 0)),
            four,
            four,
            pl.BlockSpec((total, size), lambda i: (0, head)),
        ],
        out_specs=[flat, flat, flat],
        compiler_params=params(),
        cost_estimate=cost(16 * total * total * size, 4e6),
        name="attend",
    )(gates, qo, kv, part)


def write_kernel(kv_ref, later_ref, *refs):
    heads, padded, size = later_ref.shape
    parts, out_ref = refs[:-1], refs[-1]
    groups, _, rows, _ = out_ref.shape
    for head in range(heads):
        columns = pl.ds(head * size, size)
        dq_ref, dk_ref, dv_ref = parts[3 * head : 3 * head + 3]
        key = rows_of(kv_ref[:, 0, :, columns]).astype(F32)
        value = rows_of(kv_ref[:, 1, :, columns])
        later = split(later_ref[head, :size, :])
        later_normal = later_ref[head, size : size + 1, :]
        features, slopes = feature_map(key)
        high, low = later
        grad_features = dot(value, high, 1, 1) + dot(value, low, 1, 1) + later_normal
        grad_key = dk_ref[...] + grad_features * slopes
        grad_value = dv_ref[...] + dot3(split(features), later)
        out_ref[:, 0, :, columns] = dq_ref[...].reshape(groups, rows, size)
        out_ref[:, 1, :, columns] = grad_key.astype(BF16).reshape(groups, rows, size)
        out_ref[:, 2, :, columns] = grad_value.astype(BF16).reshape(groups, rows, size)


def memory_write(kv, later, parts):
    groups, _, rows, width = kv.shape
    heads, padded, size = later.shape
    return pl.pallas_call(
        write_kernel,
        out_shape=jax.ShapeDtypeStruct((groups, 3, rows, width), BF16),
        compiler_params=params(),
        cost_estimate=cost(heads * 5 * 2 * groups * rows * size * size * 2, 4e6),
        name="memory_write",
    )(kv, later, *parts)


def later_sums(sums, rows, columns):
    me = lax.axis_index("seq")
    second = me % 2 == 1
    line = 2 * columns

    def send(value, pairs):
        return lax.ppermute(value, "seq", pairs)

    def swap(value):
        return send(value, [(i, i ^ 1) for i in range(rows * line)])

    mine = jnp.where(second, sums[1], sums[0])
    other = jnp.where(second, sums[0], sums[1])
    received = swap(other)
    chip = mine + received
    below = None
    step = 1
    while step < rows:
        sent = chip if below is None else chip + below
        got = send(sent, [(i, i - step * line) for i in range(step * line, rows * line)])
        below = got if below is None else below + got
        step *= 2
    column = (me // 2) % columns
    whole = chip + below
    later = below
    for shift in range(1, columns):
        value = jnp.where(column >= shift, whole, below)
        pairs = [
            ((r * columns + c) * 2 + k, (r * columns + (c - shift) % columns) * 2 + k)
            for r in range(rows)
            for c in range(columns)
            for k in range(2)
        ]
        later = later + send(value, pairs)
    returned = swap(jnp.where(second, later + mine, later))
    kept = jnp.where(second, later, later + received)
    return jnp.where(second, jnp.stack([returned, kept]), jnp.stack([kept, returned]))


def exchange(array):
    return lax.all_to_all(array, "tok", split_axis=0, concat_axis=0, tiled=True)


def body(queries, key_vectors, value_vectors, grad_output, memory, normalizer, gate_logit):
    groups = lax.axis_size("tok")
    heads = gate_logit.shape[0] // groups
    gates = jax.nn.sigmoid(
        lax.dynamic_slice_in_dim(gate_logit, lax.axis_index("tok") * heads, heads)
    )[None, :]
    qo = exchange(pack([queries, grad_output], groups))
    kv = exchange(pack([key_vectors, value_vectors], groups))
    sums, part = memory_read(gates, qo, memory[0], normalizer[0][:, None, :])
    later = later_sums(sums, *SEQ_GRID)
    parts = [value for head in range(heads) for value in attend(head, gates, qo, kv, part)]
    return tuple(unpack(exchange(memory_write(kv, later, parts))))


def solution(mesh):
    in_specs = (
        P(("seq", "tok"), None),
        P(("seq", "tok"), None),
        P(("seq", "tok"), None),
        P(("seq", "tok"), None),
        P("seq", "tok", None, None),
        P("seq", "tok", None),
        P(),
    )
    out_specs = (P(("seq", "tok"), None), P(("seq", "tok"), None), P(("seq", "tok"), None))
    return jax.shard_map(body, mesh=mesh, in_specs=in_specs, out_specs=out_specs, check_vma=False)
```

```python
import functools

import jax
import jax.numpy as jnp
from jax import lax
from jax.experimental import pallas as pl
from jax.experimental.pallas import tpu as pltpu
from jax.sharding import PartitionSpec as P

SEQ_GRID = (8, 4)
LOG2E = 1.4426950408889634
VMEM_LIMIT = 24 * 1024 * 1024
F32 = jnp.float32
BF16 = jnp.bfloat16


def params():
    return pltpu.CompilerParams(vmem_limit_bytes=VMEM_LIMIT)


def cost(flops, moved):
    return pl.CostEstimate(flops=int(flops), bytes_accessed=int(moved), transcendentals=0)


def split(value):
    high = value.astype(BF16)
    return high, (value - high.astype(F32)).astype(BF16)


def dot(left, right, left_dim=1, right_dim=0):
    return lax.dot_general(
        left, right, (((left_dim,), (right_dim,)), ((), ())), preferred_element_type=F32
    )


def dot3(left, right, left_dim=1, right_dim=0):
    (lh, ll), (rh, rl) = left, right
    return (
        dot(lh, rh, left_dim, right_dim)
        + dot(lh, rl, left_dim, right_dim)
        + dot(ll, rh, left_dim, right_dim)
    )


def feature_map(inputs):
    lower = jnp.exp(jnp.minimum(inputs, 0.0))
    positive = inputs > 0
    return jnp.where(positive, inputs + 1.0, lower), jnp.where(positive, 1.0, lower)


def gate_of(gates_ref, head):
    gates = gates_ref[...]
    at = lax.broadcasted_iota(jnp.int32, gates.shape, 1) == head
    return jnp.sum(jnp.where(at, gates, 0.0), axis=1, keepdims=True)


def rows_of(block):
    return block.reshape(block.shape[0] * block.shape[1], block.shape[2])


def pack_kernel(count, *refs):
    sources, (target, sems) = refs[:count], refs[count:]
    groups, _, _, width = target.shape
    copies = []
    for group in range(groups):
        for which, source in enumerate(sources):
            copies.append(
                pltpu.make_async_copy(
                    source.at[:, pl.ds(group * width, width)],
                    target.at[group, which],
                    sems.at[group * count + which],
                )
            )
    for copy in copies:
        copy.start()
    for copy in copies:
        copy.wait()


def pack(arrays, groups):
    rows, columns = arrays[0].shape
    count = len(arrays)
    return pl.pallas_call(
        functools.partial(pack_kernel, count),
        out_shape=jax.ShapeDtypeStruct((groups, count, rows, columns // groups), arrays[0].dtype),
        in_specs=[pl.BlockSpec(memory_space=pl.ANY)] * count,
        out_specs=pl.BlockSpec(memory_space=pltpu.VMEM),
        scratch_shapes=[pltpu.SemaphoreType.DMA((groups * count,))],
        cost_estimate=cost(0, 4 * count * rows * columns),
        name="pack",
    )(*arrays)


def unpack_kernel(count, source, *refs):
    targets, sems = refs[:count], refs[count]
    groups, _, _, width = source.shape
    copies = []
    for group in range(groups):
        for which, target in enumerate(targets):
            copies.append(
                pltpu.make_async_copy(
                    source.at[group, which],
                    target.at[:, pl.ds(group * width, width)],
                    sems.at[group * count + which],
                )
            )
    for copy in copies:
        copy.start()
    for copy in copies:
        copy.wait()


def unpack(array):
    groups, count, rows, width = array.shape
    return pl.pallas_call(
        functools.partial(unpack_kernel, count),
        out_shape=[jax.ShapeDtypeStruct((rows, groups * width), array.dtype)] * count,
        in_specs=[pl.BlockSpec(array.shape, lambda: (0, 0, 0, 0))],
        out_specs=[pl.BlockSpec(memory_space=pl.ANY)] * count,
        scratch_shapes=[pltpu.SemaphoreType.DMA((groups * count,))],
        cost_estimate=cost(0, 4 * array.size),
        name="unpack",
    )(array)


def read_kernel(gates_ref, both_ref, memory_ref, normal_ref, sums_ref, part_ref):
    gate = gate_of(gates_ref, pl.program_id(0))
    query = rows_of(both_ref[:, 0]).astype(F32)
    grad = rows_of(both_ref[:, 1]).astype(F32)
    memory = memory_ref[0]
    normal = normal_ref[0]
    size = memory.shape[0]
    features, slopes = feature_map(query)
    features2 = split(features)
    memory2 = split(memory)
    numerator = dot3(features2, memory2)
    inverse = 1.0 / jnp.sum(features * normal, axis=1, keepdims=True)
    scaled = gate * grad
    grad_numerator = scaled * inverse
    grad_denominator = -jnp.sum(scaled * numerator, axis=1, keepdims=True) * inverse * inverse
    numerator2 = split(grad_numerator)
    sums_ref[0, :size, :] = dot3(features2, numerator2, 0, 0)
    normal_grad = jnp.sum(features * grad_denominator, axis=0, keepdims=True)
    sums_ref[0, size:, :] = jnp.broadcast_to(normal_grad, (8, size))
    part_ref[...] = (dot3(numerator2, memory2, 1, 1) + grad_denominator * normal) * slopes


def memory_read(gates, both, memory, normalizer):
    groups, _, rows, width = both.shape
    heads, size, _ = memory.shape
    return pl.pallas_call(
        read_kernel,
        grid=(heads,),
        out_shape=[
            jax.ShapeDtypeStruct((heads, size + 8, size), F32),
            jax.ShapeDtypeStruct((groups * rows, width), F32),
        ],
        in_specs=[
            pl.BlockSpec(gates.shape, lambda i: (0, 0)),
            pl.BlockSpec((groups, 2, rows, size), lambda h: (0, 0, 0, h)),
            pl.BlockSpec((1, size, size), lambda h: (h, 0, 0)),
            pl.BlockSpec((1, 1, size), lambda h: (h, 0, 0)),
        ],
        out_specs=[
            pl.BlockSpec((1, size + 8, size), lambda h: (h, 0, 0)),
            pl.BlockSpec((groups * rows, size), lambda h: (0, h)),
        ],
        compiler_params=params(),
        cost_estimate=cost(heads * 9 * 2 * groups * rows * size * size * 2, 4e6),
        name="memory_read",
    )(gates, both, memory, normalizer)


def attend_kernel(block, head, gates_ref, qo_ref, kv_ref, part_ref, dq_ref, dk_ref, dv_ref):
    local_share = 1.0 - gate_of(gates_ref, head)
    query = rows_of(qo_ref[:, 0])
    grad = rows_of(qo_ref[:, 1])
    key = rows_of(kv_ref[:, 0])
    value = rows_of(kv_ref[:, 1])
    total, size = query.shape
    scale = size**-0.5
    for start in range(0, total, block):
        count = start + block
        q = query[start:count]
        o = grad[start:count]
        k = key[:count]
        scores = dot(k, q, 1, 1)
        diagonal = scores[start:]
        keep = lax.broadcasted_iota(jnp.int32, diagonal.shape, 0) <= lax.broadcasted_iota(
            jnp.int32, diagonal.shape, 1
        )
        diagonal = jnp.where(keep, diagonal, -1e30)
        scores = jnp.concatenate([scores[:start], diagonal], axis=0) if start else diagonal
        highest = jnp.max(scores, axis=0, keepdims=True)
        factor = scale * LOG2E
        weights = jnp.exp2(scores * factor - highest * factor)
        inverse = 1.0 / jnp.sum(weights, axis=0, keepdims=True)
        moved = dot(value[:count], o, 1, 1)
        centre = jnp.sum(weights * moved, axis=0, keepdims=True) * inverse
        attention = (weights * inverse).astype(BF16)
        grad_scores = (weights * (inverse * local_share) * (moved - centre)).astype(BF16)
        grad_query = dot(grad_scores, k, 0, 0)
        dq_ref[start:count, :] = (scale * grad_query + part_ref[start:count, :]).astype(BF16)
        grad_key = scale * dot(grad_scores, q)
        grad_value = local_share * dot(attention, o)
        if start:
            dk_ref[:start, :] += grad_key[:start]
            dv_ref[:start, :] += grad_value[:start]
        dk_ref[start:count, :] = grad_key[start:]
        dv_ref[start:count, :] = grad_value[start:]


def attend(head, gates, qo, kv, part):
    groups, _, rows, width = qo.shape
    total = groups * rows
    size = width // gates.shape[1]
    four = pl.BlockSpec((groups, 2, rows, size), lambda i: (0, 0, 0, head))
    flat = pl.BlockSpec((total, size), lambda i: (0, 0))
    return pl.pallas_call(
        functools.partial(attend_kernel, min(256, total), head),
        grid=(1,),
        out_shape=[
            jax.ShapeDtypeStruct((total, size), BF16),
            jax.ShapeDtypeStruct((total, size), F32),
            jax.ShapeDtypeStruct((total, size), F32),
        ],
        in_specs=[
            pl.BlockSpec(gates.shape, lambda i: (0, 0)),
            four,
            four,
            pl.BlockSpec((total, size), lambda i: (0, head)),
        ],
        out_specs=[flat, flat, flat],
        compiler_params=params(),
        cost_estimate=cost(16 * total * total * size, 4e6),
        name="attend",
    )(gates, qo, kv, part)


def write_kernel(kv_ref, later_ref, *refs):
    heads, padded, size = later_ref.shape
    parts, out_ref = refs[:-1], refs[-1]
    groups, _, rows, _ = out_ref.shape
    for head in range(heads):
        columns = pl.ds(head * size, size)
        dq_ref, dk_ref, dv_ref = parts[3 * head : 3 * head + 3]
        key = rows_of(kv_ref[:, 0, :, columns]).astype(F32)
        value = rows_of(kv_ref[:, 1, :, columns])
        later = split(later_ref[head, :size, :])
        later_normal = later_ref[head, size : size + 1, :]
        features, slopes = feature_map(key)
        high, low = later
        grad_features = dot(value, high, 1, 1) + dot(value, low, 1, 1) + later_normal
        grad_key = dk_ref[...] + grad_features * slopes
        grad_value = dv_ref[...] + dot3(split(features), later)
        out_ref[:, 0, :, columns] = dq_ref[...].reshape(groups, rows, size)
        out_ref[:, 1, :, columns] = grad_key.astype(BF16).reshape(groups, rows, size)
        out_ref[:, 2, :, columns] = grad_value.astype(BF16).reshape(groups, rows, size)


def memory_write(kv, later, parts):
    groups, _, rows, width = kv.shape
    heads, padded, size = later.shape
    return pl.pallas_call(
        write_kernel,
        out_shape=jax.ShapeDtypeStruct((groups, 3, rows, width), BF16),
        compiler_params=params(),
        cost_estimate=cost(heads * 5 * 2 * groups * rows * size * size * 2, 4e6),
        name="memory_write",
    )(kv, later, *parts)


def later_sums(sums, rows, columns):
    me = lax.axis_index("seq")
    second = me % 2 == 1
    line = 2 * columns

    def send(value, pairs):
        return lax.ppermute(value, "seq", pairs)

    def swap(value):
        return send(value, [(i, i ^ 1) for i in range(rows * line)])

    mine = jnp.where(second, sums[1], sums[0])
    other = jnp.where(second, sums[0], sums[1])
    received = swap(other)
    chip = mine + received
    below = None
    step = 1
    while step < rows:
        sent = chip if below is None else chip + below
        got = send(sent, [(i, i - step * line) for i in range(step * line, rows * line)])
        below = got if below is None else below + got
        step *= 2
    column = (me // 2) % columns
    whole = chip + below
    later = below
    for shift in sorted(range(1, columns), key=lambda k: -min(k, columns - k)):
        value = jnp.where(column >= shift, whole, below)
        pairs = [
            ((r * columns + c) * 2 + k, (r * columns + (c - shift) % columns) * 2 + k)
            for r in range(rows)
            for c in range(columns)
            for k in range(2)
        ]
        later = later + send(value, pairs)
    returned = swap(jnp.where(second, later + mine, later))
    kept = jnp.where(second, later, later + received)
    return jnp.where(second, jnp.stack([returned, kept]), jnp.stack([kept, returned]))


def exchange(array):
    return lax.all_to_all(array, "tok", split_axis=0, concat_axis=0, tiled=True)


def body(queries, key_vectors, value_vectors, grad_output, memory, normalizer, gate_logit):
    groups = lax.axis_size("tok")
    heads = gate_logit.shape[0] // groups
    gates = jax.nn.sigmoid(
        lax.dynamic_slice_in_dim(gate_logit, lax.axis_index("tok") * heads, heads)
    )[None, :]
    qo = exchange(pack([queries, grad_output], groups))
    kv = exchange(pack([key_vectors, value_vectors], groups))
    sums, part = memory_read(gates, qo, memory[0], normalizer[0][:, None, :])
    later = later_sums(sums, *SEQ_GRID)
    parts = [value for head in range(heads) for value in attend(head, gates, qo, kv, part)]
    return tuple(unpack(exchange(memory_write(kv, later, parts))))


def solution(mesh):
    in_specs = (
        P(("seq", "tok"), None),
        P(("seq", "tok"), None),
        P(("seq", "tok"), None),
        P(("seq", "tok"), None),
        P("seq", "tok", None, None),
        P("seq", "tok", None),
        P(),
    )
    out_specs = (P(("seq", "tok"), None), P(("seq", "tok"), None), P(("seq", "tok"), None))
    return jax.shard_map(body, mesh=mesh, in_specs=in_specs, out_specs=out_specs, check_vma=False)
```
